32 devices in a mesh: py: 8 (over z, x), pz: 4 (over y, core).
Axes of the slice: x: 2, y: 2, z: 4, core: 2. Of those that a mesh axis runs over, the one named last changes fastest.
Arguments:
- velocity: float32 [3, 288, 160, 2048], P(None, 'pz', 'py'), may hold values from -40 to 40
Outputs:
- filtered_velocity: float32 [3, 32, 16, 256], P(None, None, 'pz', 'py')
- stresses: float32 [6, 32, 16, 256], P(None, None, 'pz', 'py')
The draws below stay inside these ranges and needn't reach their ends.
All inputs are finite; a program needn't handle non-finite values.
Results may differ from the reference program's by a relative error of at most 0.00007.
Values sent between devices are 32-bit elements; how exact they have to be, the bound alone decides.
A program may use at most 192 MiB of HBM per device.

```python
import math
import jax
import jax.numpy as jnp
from jax import lax

NX = 2048
OZ = 32
OX = 256
OY = 16
YIN = 160
ZIN = 288


def draw_velocity(key, part):
    keys = jax.random.split(key, 6)
    shape_full = (3, ZIN, YIN, NX)
    noise = jax.random.truncated_normal(keys[0], -5.0, 5.0, shape_full, jnp.float32)
    x_pos = jnp.arange(NX).astype(jnp.float32)
    y_pos = jnp.arange(YIN).astype(jnp.float32)
    z_pos = jnp.arange(ZIN).astype(jnp.float32)
    waves = jax.random.randint(keys[1], (3, 4, 3), 1, 5).astype(jnp.float32)
    phases = jax.random.uniform(keys[2], (3, 4, 3), jnp.float32, -math.pi, math.pi)
    amplitude = jax.random.uniform(keys[3], (3, 4), jnp.float32, 0.25, 0.5)
    env_waves = jax.random.randint(keys[4], (3,), 1, 4).astype(jnp.float32)
    env_phases = jax.random.uniform(keys[5], (3,), jnp.float32, -math.pi, math.pi)
    two_pi = 2.0 * math.pi
    envelope = jnp.exp(0.5 * (jnp.cos(two_pi * env_waves[0] * x_pos / NX + env_phases[0])[None, None, :] + jnp.cos(two_pi * env_waves[1] * y_pos / 256.0 + env_phases[1])[None, :, None] + jnp.cos(two_pi * env_waves[2] * z_pos / 256.0 + env_phases[2])[:, None, None]))
    components = []
    for comp_index in range(3):
        smooth = jnp.zeros((ZIN, YIN, NX), jnp.float32)
        for mode_index in range(4):
            wave_x = jnp.cos(two_pi * waves[comp_index, mode_index, 0] * x_pos / NX + phases[comp_index, mode_index, 0])
            wave_y = jnp.cos(two_pi * waves[comp_index, mode_index, 1] * y_pos / 256.0 + phases[comp_index, mode_index, 1])
            wave_z = jnp.cos(two_pi * waves[comp_index, mode_index, 2] * z_pos / 256.0 + phases[comp_index, mode_index, 2])
            smooth = smooth + amplitude[comp_index, mode_index] * wave_z[:, None, None] * wave_y[None, :, None] * wave_x[None, None, :]
        rough = noise[comp_index] + 0.6 * noise[(comp_index + 1) % 3]
        components.append(smooth + envelope * rough)
    return jnp.stack(components).astype(jnp.float32)


def setup_inputs(seed: int = 0) -> dict:
    seeds = jax.random.split(jax.random.key(seed), 2)
    velocity = draw_velocity(jax.random.fold_in(seeds[1], 71), 0)
    return dict(velocity=velocity)


spread_cells = 8.0
stress_pairs = ((0, 0), (0, 1), (0, 2), (1, 1), (1, 2), (2, 2))


def gauss_taps():
    offsets = jnp.arange(-16, 17).astype(jnp.float32)
    raw_taps = jnp.exp(-offsets * offsets / (2.0 * spread_cells * spread_cells))
    return raw_taps / jnp.sum(raw_taps)


def reference(velocity):
    taps = gauss_taps()

    def one_plane(plane_index):
        plane = lax.dynamic_index_in_dim(velocity, plane_index, 1, keepdims=False)
        products = jnp.stack([plane[first_comp] * plane[second_comp] for first_comp, second_comp in stress_pairs])
        fields = jnp.concatenate([plane, products], axis=0)
        extended = jnp.concatenate([fields[:, :, NX - 16:], fields, fields[:, :, :16]], axis=2)
        x_sum = jnp.zeros((9, YIN, OX), jnp.float32)
        for offset in range(-16, 17):
            x_sum = x_sum + taps[offset + 16] * extended[:, :, 16 + offset:16 + offset + 8 * OX:8]
        y_sum = jnp.zeros((9, OY, OX), jnp.float32)
        for offset in range(-16, 17):
            y_sum = y_sum + taps[offset + 16] * x_sum[:, 16 + offset:16 + offset + 8 * OY:8, :]
        return y_sum

    stacked = lax.map(one_plane, jnp.arange(ZIN).astype(jnp.int32))
    z_sum = jnp.zeros((OZ, 9, OY, OX), jnp.float32)
    for offset in range(-16, 17):
        z_sum = z_sum + taps[offset + 16] * stacked[16 + offset:16 + offset + 8 * OZ:8]
    filtered = jnp.transpose(z_sum, (1, 0, 2, 3))
    filtered_velocity = filtered[0:3]
    stresses = jnp.stack([filtered[3 + pair_index] - filtered[first_comp] * filtered[second_comp] for pair_index, (first_comp, second_comp) in enumerate(stress_pairs)])
    return filtered_velocity, stresses
```

```python
import functools
import numpy as np
import ml_dtypes
import jax
import jax.numpy as jnp
from jax import lax
from jax.sharding import PartitionSpec as P
from jax.experimental import pallas as pl
from jax.experimental.pallas import tpu as pltpu

stress_pairs = ((0, 0), (0, 1), (0, 2), (1, 1), (1, 2), (2, 2))
f32, bf16 = jnp.float32, jnp.bfloat16


def tap(t):
    r = np.arange(-16, 17).astype(np.float64)
    s = np.sum(np.exp(-r * r / 128.0))
    t = np.asarray(t, np.float64)
    return np.where(np.abs(t) <= 16, np.exp(-t * t / 128.0) / s, 0.0)


class Plan:
    def __init__(self, shape, npy, npz):
        _, self.zl, self.yl, self.nx = shape
        self.npy, self.npz = npy, npz
        zl, yl = self.zl, self.yl
        self.oz = (zl * npz - 32) // 8
        self.oy = (yl * npy - 32) // 8
        self.ox = self.nx // 8
        self.kb = self.ox // npy
        self.jq = self.oy // npz
        self.pk = 128 // self.kb
        self.cz = max(c for c in range(1, 9) if zl % c == 0)
        self.nch = zl // self.cz
        self.yp = -(-yl // 8) * 8
        self.kk = self.cz * self.yp
        cz, nch = self.cz, self.nch
        base = lambda s: (s + 7) // 8 - 4
        self.base_p = [base(zl * p) for p in range(npz)]
        starts = np.array([[zl * p + cz * c for c in range(nch)] for p in range(npz)])
        bases = base(starts)
        self.nic = int(np.max((starts + cz - 1) // 8 - bases + 1))
        self.offs = bases - bases[:, :1]
        self.ni = int(self.offs.max()) + self.nic
        self.groups = -(-self.ni // self.pk)
        z = starts[:, :, None, None] + np.arange(cz)[None, None, None, :]
        i = bases[:, :, None, None] + np.arange(8)[None, None, :, None]
        az = np.where((i >= 0) & (i < self.oz), tap(z - 16 - 8 * i), 0.0)
        az[:, :, self.nic:] = 0.0
        self.az = np.repeat(az, self.yp, axis=3).astype(np.float32)
        ay = np.zeros((npy, 8, self.yp))
        self.mask = np.zeros((npy, self.oy // 8, 8), np.float32)
        for d in range(npy):
            y = yl * d + np.arange(yl)
            for j in range(self.oy):
                w = tap(y - 16 - 8 * j)
                if np.any(w != 0):
                    ay[d, j % 8, :yl] += w
                    self.mask[d, j // 8, j % 8] = 1.0
        assert self.mask.sum(axis=1).max() == 1
        self.ay = np.tile(ay, (1, 1, cz)).astype(np.float32)
        n = np.arange(self.nx)[:, None]
        k = np.arange(self.ox)[None, :]
        t = (n - 8 * k + self.nx // 2) % self.nx - self.nx // 2
        wx = tap(t).astype(np.float32)
        self.wx_hi = wx.astype(ml_dtypes.bfloat16)
        self.wx_lo = (wx - self.wx_hi.astype(np.float32)).astype(ml_dtypes.bfloat16)


def split(val):
    hi = val.astype(bf16)
    return hi, (val - hi.astype(f32)).astype(bf16)


def dot(a, b):
    return jnp.dot(a, b, preferred_element_type=f32)


def sum_block(pn, c, p, d, v_ref, az_ref, ay_ref, acc):
    xt = 256
    wz = az_ref[p, c][: pn.nic]
    wy = ay_ref[d]
    w = (wz[:, None, :] * wy[None, :, :]).reshape(pn.nic * 8, pn.kk)
    w_hi = w.astype(bf16).astype(f32)
    w2 = jnp.concatenate([w_hi, w - w_hi], axis=0).astype(bf16)
    off = (pn.zl * p + pn.cz * c + 7) // 8 - (pn.zl * p + 7) // 8
    m = pn.nic * 8

    def tile(x, carry):
        xs = pl.ds(pl.multiple_of(x * xt, xt), xt)
        comps = []
        for a in range(3):
            blk = v_ref[a, :, :, xs]
            if pn.yp > pn.yl:
                blk = jnp.concatenate([blk, jnp.zeros((pn.cz, pn.yp - pn.yl, xt), f32)], axis=1)
            comps.append(blk.reshape(pn.kk, xt))
        for f in range(9):
            if f < 3:
                val = comps[f]
            else:
                a, b = stress_pairs[f - 3]
                val = comps[a] * comps[b]
            hi, lo = split(val)
            r = dot(w2, hi) + dot(w2, lo)
            r = (r[:m] + r[m:]).reshape(pn.nic, 8, xt)
            acc[f, pl.ds(off, pn.nic), :, xs] += r
        return carry

    lax.fori_loop(0, pn.nx // xt, tile, 0)


def first_group(pn, g, acc, wh_ref, wl_ref, out_ref):
    rows = min(pn.pk, pn.ni - g * pn.pk)
    parts = []
    for q in range(rows):
        a = acc[:, g * pn.pk + q].reshape(72, pn.nx)
        hi, lo = split(a)
        parts.append(dot(hi, wh_ref[...]) + (dot(lo, wh_ref[...]) + dot(hi, wl_ref[...])))
    lane = lax.broadcasted_iota(jnp.int32, (72, 128), 1)
    for m in range(pn.npy):
        mg, mo = divmod(m * pn.kb, 128)
        res = jnp.zeros((72, 128), f32)
        for q in range(rows):
            piece = parts[q][:, mg * 128:(mg + 1) * 128]
            shift = (q * pn.kb - mo) % 128
            if shift:
                piece = pltpu.roll(piece, shift, 1)
            res = jnp.where((lane >= q * pn.kb) & (lane < (q + 1) * pn.kb), piece, res)
        out_ref[m, g] = res.reshape(9, 8, 128)


def local_kernel(pn, v_ref, az_ref, ay_ref, wh_ref, wl_ref, out_ref, acc):
    c = pl.program_id(0)
    d, p = lax.axis_index("py"), lax.axis_index("pz")

    @pl.when(c == 0)
    def _():
        acc[...] = jnp.zeros_like(acc)

    sum_block(pn, c, p, d, v_ref, az_ref, ay_ref, acc)

    @pl.when(c == pn.nch - 1)
    def _():
        for g in range(pn.groups):
            first_group(pn, g, acc, wh_ref, wl_ref, out_ref)


def local_sums(pn, velocity):
    whole = lambda a: pl.BlockSpec(a.shape, lambda c: (0,) * a.ndim)
    tables = [pn.az, pn.ay, pn.wx_hi, pn.wx_lo]
    return pl.pallas_call(
        functools.partial(local_kernel, pn),
        grid=(pn.nch,),
        in_specs=[pl.BlockSpec((3, pn.cz, pn.yl, pn.nx), lambda c: (0, c, 0, 0))] + [whole(t) for t in tables],
        out_specs=pl.BlockSpec((pn.npy, pn.groups, 9, 8, 128), lambda c: (0, 0, 0, 0, 0)),
        out_shape=jax.ShapeDtypeStruct((pn.npy, pn.groups, 9, 8, 128), f32),
        scratch_shapes=[pltpu.VMEM((9, pn.ni, 8, pn.nx), f32)],
        compiler_params=pltpu.CompilerParams(vmem_limit_bytes=50 * 2**20),
    )(velocity, *[jnp.asarray(t) for t in tables])


def on_device(npy, npz, velocity):
    pn = Plan(velocity.shape, npy, npz)
    packed = local_sums(pn, velocity)
    moved = lax.all_to_all(packed, "py", split_axis=0, concat_axis=0, tiled=True)
    mask = pn.mask[:, :, None, None, :, None]
    rows = jnp.sum(jnp.where(mask > 0, moved[:, None], 0.0), axis=0)
    rows = jnp.transpose(rows, (0, 3, 1, 2, 4)).reshape(npz, pn.jq, pn.groups, 9, 128)
    planes = lax.all_to_all(rows, "pz", split_axis=0, concat_axis=0, tiled=True)
    planes = planes.reshape(npz, pn.jq, pn.groups, 9, pn.pk, pn.kb)
    planes = jnp.transpose(planes, (0, 3, 2, 4, 1, 5)).reshape(npz, 9, pn.groups * pn.pk, pn.jq, pn.kb)
    total = 0.0
    for p in range(npz):
        lo = pn.base_p[p]
        i0, i1 = max(lo, 0), min(lo + pn.ni, pn.oz)
        total = total + jnp.pad(
            planes[p][:, i0 - lo:i1 - lo], ((0, 0), (i0, pn.oz - i1), (0, 0), (0, 0))
        )
    stresses = jnp.stack([total[3 + n] - total[a] * total[b] for n, (a, b) in enumerate(stress_pairs)])
    return total[:3], stresses


def solution(mesh):
    return jax.shard_map(
        functools.partial(on_device, mesh.shape["py"], mesh.shape["pz"]),
        mesh=mesh,
        in_specs=(P(None, "pz", "py", None),),
        out_specs=(P(None, None, "pz", "py"), P(None, None, "pz", "py")),
        check_vma=False,
    )
```

```python
import functools
import numpy as np
import ml_dtypes
import jax
import jax.numpy as jnp
from jax import lax
from jax.sharding import PartitionSpec as P
from jax.experimental import pallas as pl
from jax.experimental.pallas import tpu as pltpu

stress_pairs = ((0, 0), (0, 1), (0, 2), (1, 1), (1, 2), (2, 2))
f32, bf16 = jnp.float32, jnp.bfloat16


def tap(t):
    r = np.arange(-16, 17).astype(np.float64)
    s = np.sum(np.exp(-r * r / 128.0))
    t = np.asarray(t, np.float64)
    return np.where(np.abs(t) <= 16, np.exp(-t * t / 128.0) / s, 0.0)


class Plan:
    def __init__(self, shape, npy, npz):
        _, self.zl, self.yl, self.nx = shape
        self.npy, self.npz = npy, npz
        zl, yl = self.zl, self.yl
        self.oz = (zl * npz - 32) // 8
        self.oy = (yl * npy - 32) // 8
        self.ox = self.nx // 8
        self.kb = self.ox // npy
        self.jq = self.oy // npz
        self.pk = 128 // self.kb
        self.cz = 8 if zl % 8 == 0 else zl
        self.nch = zl // self.cz
        self.zp = -(-self.cz // 8) * 8
        self.kk = yl * self.zp
        cz, nch = self.cz, self.nch
        base = lambda s: (s + 7) // 8 - 4
        self.base_p = [base(zl * p) for p in range(npz)]
        starts = np.array([[zl * p + cz * c for c in range(nch)] for p in range(npz)])
        bases = base(starts)
        self.nic = int(np.max((starts + cz - 1) // 8 - bases + 1))
        self.offs = bases - bases[:, :1]
        self.ni = int(self.offs.max()) + self.nic
        self.groups = -(-self.ni // self.pk)
        z = starts[:, :, None, None] + np.arange(cz)[None, None, None, :]
        i = bases[:, :, None, None] + np.arange(8)[None, None, :, None]
        az = np.where((i >= 0) & (i < self.oz), tap(z - 16 - 8 * i), 0.0)
        az[:, :, self.nic:] = 0.0
        az = np.pad(az, ((0, 0), (0, 0), (0, 0), (0, self.zp - cz)))
        self.az = np.tile(az, (1, 1, 1, yl)).astype(np.float32)
        ay = np.zeros((npy, 8, yl))
        self.mask = np.zeros((npy, self.oy // 8, 8), np.float32)
        for d in range(npy):
            y = yl * d + np.arange(yl)
            for j in range(self.oy):
                w = tap(y - 16 - 8 * j)
                if np.any(w != 0):
                    ay[d, j % 8] += w
                    self.mask[d, j // 8, j % 8] = 1.0
        assert self.mask.sum(axis=1).max() == 1
        self.ay = np.repeat(ay, self.zp, axis=2).astype(np.float32)
        n = np.arange(self.nx)[:, None]
        k = np.arange(self.ox)[None, :]
        t = (n - 8 * k + self.nx // 2) % self.nx - self.nx // 2
        wx = tap(t).astype(np.float32)
        self.wx_hi = wx.astype(ml_dtypes.bfloat16)
        self.wx_lo = (wx - self.wx_hi.astype(np.float32)).astype(ml_dtypes.bfloat16)


def split(val):
    hi = val.astype(bf16)
    return hi, (val - hi.astype(f32)).astype(bf16)


def dot(a, b):
    return jnp.dot(a, b, preferred_element_type=f32)


def sum_block(pn, c, p, d, v_ref, az_ref, ay_ref, acc):
    xt = 256
    wz = az_ref[p, c][: pn.nic]
    wy = ay_ref[d]
    w = (wz[:, None, :] * wy[None, :, :]).reshape(pn.nic * 8, pn.kk)
    w_hi = w.astype(bf16).astype(f32)
    w2 = jnp.concatenate([w_hi, w - w_hi], axis=0).astype(bf16)
    off = (pn.zl * p + pn.cz * c + 7) // 8 - (pn.zl * p + 7) // 8
    m = pn.nic * 8

    def tile(x, carry):
        xs = pl.ds(pl.multiple_of(x * xt, xt), xt)
        comps = []
        for a in range(3):
            blk = v_ref[a, :, :, xs]
            if pn.zp > pn.cz:
                blk = jnp.concatenate([blk, jnp.zeros((pn.yl, pn.zp - pn.cz, xt), f32)], axis=1)
            comps.append(blk.reshape(pn.kk, xt))
        for f in range(9):
            if f < 3:
                val = comps[f]
            else:
                a, b = stress_pairs[f - 3]
                val = comps[a] * comps[b]
            hi, lo = split(val)
            r = dot(w2, hi) + dot(w2, lo)
            r = (r[:m] + r[m:]).reshape(pn.nic, 8, xt)
            acc[f, pl.ds(off, pn.nic), :, xs] += r
        return carry

    lax.fori_loop(0, pn.nx // xt, tile, 0)


def first_group(pn, g, acc, wh_ref, wl_ref, out_ref):
    rows = min(pn.pk, pn.ni - g * pn.pk)
    parts = []
    for q in range(rows):
        a = acc[:, g * pn.pk + q].reshape(72, pn.nx)
        hi, lo = split(a)
        parts.append(dot(hi, wh_ref[...]) + (dot(lo, wh_ref[...]) + dot(hi, wl_ref[...])))
    lane = lax.broadcasted_iota(jnp.int32, (72, 128), 1)
    for m in range(pn.npy):
        mg, mo = divmod(m * pn.kb, 128)
        res = jnp.zeros((72, 128), f32)
        for q in range(rows):
            piece = parts[q][:, mg * 128:(mg + 1) * 128]
            shift = (q * pn.kb - mo) % 128
            if shift:
                piece = pltpu.roll(piece, shift, 1)
            res = jnp.where((lane >= q * pn.kb) & (lane < (q + 1) * pn.kb), piece, res)
        out_ref[m, g] = res.reshape(9, 8, 128)


def local_kernel(pn, v_ref, az_ref, ay_ref, wh_ref, wl_ref, out_ref, acc):
    c = pl.program_id(0)
    d, p = lax.axis_index("py"), lax.axis_index("pz")

    @pl.when(c == 0)
    def _():
        acc[...] = jnp.zeros_like(acc)

    sum_block(pn, c, p, d, v_ref, az_ref, ay_ref, acc)

    @pl.when(c == pn.nch - 1)
    def _():
        for g in range(pn.groups):
            first_group(pn, g, acc, wh_ref, wl_ref, out_ref)


def local_sums(pn, velocity):
    whole = lambda a: pl.BlockSpec(a.shape, lambda c: (0,) * a.ndim)
    tables = [pn.az, pn.ay, pn.wx_hi, pn.wx_lo]
    return pl.pallas_call(
        functools.partial(local_kernel, pn),
        grid=(pn.nch,),
        in_specs=[pl.BlockSpec((3, pn.yl, pn.cz, pn.nx), lambda c: (0, 0, c, 0))] + [whole(t) for t in tables],
        out_specs=pl.BlockSpec((pn.npy, pn.groups, 9, 8, 128), lambda c: (0, 0, 0, 0, 0)),
        out_shape=jax.ShapeDtypeStruct((pn.npy, pn.groups, 9, 8, 128), f32),
        scratch_shapes=[pltpu.VMEM((9, pn.ni, 8, pn.nx), f32)],
        compiler_params=pltpu.CompilerParams(vmem_limit_bytes=50 * 2**20),
    )(velocity, *[jnp.asarray(t) for t in tables])


def on_device(npy, npz, velocity):
    pn = Plan(velocity.shape, npy, npz)
    packed = local_sums(pn, jnp.transpose(velocity, (0, 2, 1, 3)))
    moved = lax.all_to_all(packed, "py", split_axis=0, concat_axis=0, tiled=True)
    mask = pn.mask[:, :, None, None, :, None]
    rows = jnp.sum(jnp.where(mask > 0, moved[:, None], 0.0), axis=0)
    rows = jnp.transpose(rows, (0, 3, 1, 2, 4)).reshape(npz, pn.jq, pn.groups, 9, 128)
    planes = lax.all_to_all(rows, "pz", split_axis=0, concat_axis=0, tiled=True)
    planes = planes.reshape(npz, pn.jq, pn.groups, 9, pn.pk, pn.kb)
    planes = jnp.transpose(planes, (0, 3, 2, 4, 1, 5)).reshape(npz, 9, pn.groups * pn.pk, pn.jq, pn.kb)
    total = 0.0
    for p in range(npz):
        lo = pn.base_p[p]
        i0, i1 = max(lo, 0), min(lo + pn.ni, pn.oz)
        total = total + jnp.pad(
            planes[p][:, i0 - lo:i1 - lo], ((0, 0), (i0, pn.oz - i1), (0, 0), (0, 0))
        )
    stresses = jnp.stack([total[3 + n] - total[a] * total[b] for n, (a, b) in enumerate(stress_pairs)])
    return total[:3], stresses


def solution(mesh):
    return jax.shard_map(
        functools.partial(on_device, mesh.shape["py"], mesh.shape["pz"]),
        mesh=mesh,
        in_specs=(P(None, "pz", "py", None),),
        out_specs=(P(None, None, "pz", "py"), P(None, None, "pz", "py")),
        check_vma=False,
    )
```

```python
import functools
import numpy as np
import ml_dtypes
import jax
import jax.numpy as jnp
from jax import lax
from jax.sharding import PartitionSpec as P
from jax.experimental import pallas as pl
from jax.experimental.pallas import tpu as pltpu

stress_pairs = ((0, 0), (0, 1), (0, 2), (1, 1), (1, 2), (2, 2))
f32, bf16 = jnp.float32, jnp.bfloat16


def tap(t):
    r = np.arange(-16, 17).astype(np.float64)
    s = np.sum(np.exp(-r * r / 128.0))
    t = np.asarray(t, np.float64)
    return np.where(np.abs(t) <= 16, np.exp(-t * t / 128.0) / s, 0.0)


class Plan:
    def __init__(self, shape, npy, npz):
        _, self.zl, self.yl, self.nx = shape
        self.npy, self.npz = npy, npz
        zl, yl = self.zl, self.yl
        self.oz = (zl * npz - 32) // 8
        self.oy = (yl * npy - 32) // 8
        self.ox = self.nx // 8
        self.kb = self.ox // npy
        self.jq = self.oy // npz
        self.pk = 128 // self.kb
        self.cz = 8 if zl % 8 == 0 else zl
        self.nch = zl // self.cz
        self.zp = -(-self.cz // 8) * 8
        self.kk = yl * self.zp
        cz, nch = self.cz, self.nch
        base = lambda s: (s + 7) // 8 - 4
        self.base_p = [base(zl * p) for p in range(npz)]
        starts = np.array([[zl * p + cz * c for c in range(nch)] for p in range(npz)])
        bases = base(starts)
        self.nic = int(np.max((starts + cz - 1) // 8 - bases + 1))
        self.offs = bases - bases[:, :1]
        self.ni = int(self.offs.max()) + self.nic
        self.groups = -(-self.ni // self.pk)
        z = starts[:, :, None, None] + np.arange(cz)[None, None, None, :]
        i = bases[:, :, None, None] + np.arange(8)[None, None, :, None]
        az = np.where((i >= 0) & (i < self.oz), tap(z - 16 - 8 * i), 0.0)
        az[:, :, self.nic:] = 0.0
        az = np.pad(az, ((0, 0), (0, 0), (0, 0), (0, self.zp - cz)))
        self.az = np.tile(az, (1, 1, 1, yl)).astype(np.float32)
        ay = np.zeros((npy, 8, yl))
        self.mask = np.zeros((npy, self.oy // 8, 8), np.float32)
        for d in range(npy):
            y = yl * d + np.arange(yl)
            for j in range(self.oy):
                w = tap(y - 16 - 8 * j)
                if np.any(w != 0):
                    ay[d, j % 8] += w
                    self.mask[d, j // 8, j % 8] = 1.0
        assert self.mask.sum(axis=1).max() == 1
        self.ay = np.repeat(ay, self.zp, axis=2).astype(np.float32)
        n = np.arange(self.nx)[:, None]
        k = np.arange(self.ox)[None, :]
        t = (n - 8 * k + self.nx // 2) % self.nx - self.nx // 2
        wx = tap(t).astype(np.float32)
        self.wx_hi = wx.astype(ml_dtypes.bfloat16)
        self.wx_lo = (wx - self.wx_hi.astype(np.float32)).astype(ml_dtypes.bfloat16)


def split(val):
    hi = val.astype(bf16)
    return hi, (val - hi.astype(f32)).astype(bf16)


def dot(a, b):
    return jnp.dot(a, b, preferred_element_type=f32)


def sum_block(pn, c, p, d, v_ref, az_ref, ay_ref, acc):
    xt = 256
    wz = az_ref[p, c][: pn.nic]
    wy = ay_ref[d]
    w = (wz[:, None, :] * wy[None, :, :]).reshape(pn.nic * 8, pn.kk)
    w_hi = w.astype(bf16).astype(f32)
    w2 = jnp.concatenate([w_hi, w - w_hi], axis=0).astype(bf16)
    off = (pn.zl * p + pn.cz * c + 7) // 8 - (pn.zl * p + 7) // 8
    m = pn.nic * 8

    def tile(x, carry):
        xs = pl.ds(pl.multiple_of(x * xt, xt), xt)
        comps = []
        for a in range(3):
            blk = v_ref[a, :, :, xs]
            if pn.zp > pn.cz:
                blk = jnp.concatenate([blk, jnp.zeros((pn.yl, pn.zp - pn.cz, xt), f32)], axis=1)
            comps.append(blk.reshape(pn.kk, xt))
        for f in range(9):
            if f < 3:
                val = comps[f]
            else:
                a, b = stress_pairs[f - 3]
                val = comps[a] * comps[b]
            hi, lo = split(val)
            r = dot(w2, hi) + dot(w2, lo)
            r = (r[:m] + r[m:]).reshape(pn.nic, 8, xt)
            acc[f, pl.ds(off, pn.nic), :, xs] += r
        return carry

    lax.fori_loop(0, pn.nx // xt, tile, 0)


def first_group(pn, g, acc, wh_ref, wl_ref, out_ref):
    rows = min(pn.pk, pn.ni - g * pn.pk)
    parts = []
    for q in range(rows):
        a = acc[:, g * pn.pk + q].reshape(72, pn.nx)
        hi, lo = split(a)
        parts.append(dot(hi, wh_ref[...]) + (dot(lo, wh_ref[...]) + dot(hi, wl_ref[...])))
    lane = lax.broadcasted_iota(jnp.int32, (72, 128), 1)
    for m in range(pn.npy):
        mg, mo = divmod(m * pn.kb, 128)
        res = jnp.zeros((72, 128), f32)
        for q in range(rows):
            piece = parts[q][:, mg * 128:(mg + 1) * 128]
            shift = (q * pn.kb - mo) % 128
            if shift:
                piece = pltpu.roll(piece, shift, 1)
            res = jnp.where((lane >= q * pn.kb) & (lane < (q + 1) * pn.kb), piece, res)
        out_ref[m, g] = res.reshape(9, 8, 128)


def local_kernel(pn, v_ref, az_ref, ay_ref, wh_ref, wl_ref, out_ref, acc):
    c = pl.program_id(0)
    d, p = lax.axis_index("py"), lax.axis_index("pz")

    @pl.when(c == 0)
    def _():
        acc[...] = jnp.zeros_like(acc)

    sum_block(pn, c, p, d, v_ref, az_ref, ay_ref, acc)

    @pl.when(c == pn.nch - 1)
    def _():
        for g in range(pn.groups):
            first_group(pn, g, acc, wh_ref, wl_ref, out_ref)


def local_sums(pn, velocity):
    whole = lambda a: pl.BlockSpec(a.shape, lambda c: (0,) * a.ndim)
    tables = [pn.az, pn.ay, pn.wx_hi, pn.wx_lo]
    return pl.pallas_call(
        functools.partial(local_kernel, pn),
        grid=(pn.nch,),
        in_specs=[pl.BlockSpec((3, pn.yl, pn.cz, pn.nx), lambda c: (0, 0, c, 0))] + [whole(t) for t in tables],
        out_specs=pl.BlockSpec((pn.npy, pn.groups, 9, 8, 128), lambda c: (0, 0, 0, 0, 0)),
        out_shape=jax.ShapeDtypeStruct((pn.npy, pn.groups, 9, 8, 128), f32),
        scratch_shapes=[pltpu.VMEM((9, pn.ni, 8, pn.nx), f32)],
        compiler_params=pltpu.CompilerParams(vmem_limit_bytes=50 * 2**20),
    )(velocity, *[jnp.asarray(t) for t in tables])


def exchange_kernel(pn, in_ref, vel_ref, str_ref, rec_y, snd_z, rec_z, sy, ry, sz, rz):
    d, p = lax.axis_index("py"), lax.axis_index("pz")
    npy, npz, jq, kb = pn.npy, pn.npz, pn.jq, pn.kb
    mesh_id = pl.DeviceIdType.MESH
    barrier = pltpu.get_barrier_semaphore()
    for o in range(1, npy):
        pl.semaphore_signal(barrier, inc=1, device_id=(lax.rem(d + o, npy), p), device_id_type=mesh_id)
    for o in range(1, npz):
        pl.semaphore_signal(barrier, inc=1, device_id=(d, lax.rem(p + o, npz)), device_id_type=mesh_id)
    pl.semaphore_wait(barrier, npy + npz - 2)

    copies = []
    for o in range(1, npy):
        to = lax.rem(d + o, npy)
        copies.append(pltpu.make_async_remote_copy(
            src_ref=in_ref.at[to], dst_ref=rec_y.at[d], send_sem=sy.at[o], recv_sem=ry.at[o],
            device_id=(to, p), device_id_type=mesh_id))
        copies[-1].start()
    rec_y[d] = in_ref[d]
    for copy in copies:
        copy.wait()

    row = lax.broadcasted_iota(jnp.int32, (9, 8, 128), 1)
    for g in range(pn.groups):
        for h in range(pn.oy // 8):
            total = jnp.zeros((9, 8, 128), f32)
            for s in range(npy):
                rows = np.nonzero(pn.mask[s, h])[0]
                if len(rows) == 0:
                    continue
                val = rec_y[s, g]
                if len(rows) < 8:
                    val = jnp.where((row >= int(rows[0])) & (row <= int(rows[-1])), val, 0.0)
                total = total + val
            for part in range(8 // jq):
                snd_z[h * (8 // jq) + part, g] = total[:, part * jq:(part + 1) * jq, :]

    copies = []
    for o in range(1, npz):
        to = lax.rem(p + o, npz)
        copies.append(pltpu.make_async_remote_copy(
            src_ref=snd_z.at[to], dst_ref=rec_z.at[p], send_sem=sz.at[o], recv_sem=rz.at[o],
            device_id=(d, to), device_id_type=mesh_id))
        copies[-1].start()
    rec_z[p] = snd_z[p]
    for copy in copies:
        copy.wait()

    for i in range(pn.oz):
        total = jnp.zeros((9, jq, kb), f32)
        for s in range(npz):
            n = i - pn.base_p[s]
            if 0 <= n < pn.ni:
                g, q = divmod(n, pn.pk)
                total = total + rec_z[s, g, :, :, q * kb:(q + 1) * kb]
        vel_ref[:, i] = total[:3]
        for n, (a, b) in enumerate(stress_pairs):
            str_ref[n, i] = total[3 + n] - total[a] * total[b]


def exchange(pn, packed):
    vmem = pl.BlockSpec(memory_space=pltpu.VMEM)
    zbuf = pltpu.VMEM((pn.npz, pn.groups, 9, pn.jq, 128), f32)
    sems = [pltpu.SemaphoreType.DMA((n,)) for n in (pn.npy, pn.npy, pn.npz, pn.npz)]
    return pl.pallas_call(
        functools.partial(exchange_kernel, pn),
        in_specs=[vmem],
        out_specs=(vmem, vmem),
        out_shape=tuple(jax.ShapeDtypeStruct((n, pn.oz, pn.jq, pn.kb), f32) for n in (3, 6)),
        scratch_shapes=[pltpu.VMEM((pn.npy, pn.groups, 9, 8, 128), f32), zbuf, zbuf] + sems,
        compiler_params=pltpu.CompilerParams(
            collective_id=0, has_side_effects=True, vmem_limit_bytes=32 * 2**20
        ),
    )(packed)


def on_device(npy, npz, velocity):
    pn = Plan(velocity.shape, npy, npz)
    packed = local_sums(pn, jnp.transpose(velocity, (0, 2, 1, 3)))
    return exchange(pn, packed)


def solution(mesh):
    return jax.shard_map(
        functools.partial(on_device, mesh.shape["py"], mesh.shape["pz"]),
        mesh=mesh,
        in_specs=(P(None, "pz", "py", None),),
        out_specs=(P(None, None, "pz", "py"), P(None, None, "pz", "py")),
        check_vma=False,
    )
```

```python
import functools
import numpy as np
import ml_dtypes
import jax
import jax.numpy as jnp
from jax import lax
from jax.sharding import PartitionSpec as P
from jax.experimental import pallas as pl
from jax.experimental.pallas import tpu as pltpu

stress_pairs = ((0, 0), (0, 1), (0, 2), (1, 1), (1, 2), (2, 2))
f32, bf16 = jnp.float32, jnp.bfloat16


def tap(t):
    r = np.arange(-16, 17).astype(np.float64)
    s = np.sum(np.exp(-r * r / 128.0))
    t = np.asarray(t, np.float64)
    return np.where(np.abs(t) <= 16, np.exp(-t * t / 128.0) / s, 0.0)


class Plan:
    def __init__(self, shape, npy, npz):
        _, self.zl, self.yl, self.nx = shape
        self.npy, self.npz = npy, npz
        zl, yl = self.zl, self.yl
        self.oz = (zl * npz - 32) // 8
        self.oy = (yl * npy - 32) // 8
        self.ox = self.nx // 8
        self.kb = self.ox // npy
        self.jq = self.oy // npz
        self.pk = 128 // self.kb
        self.cz = 8 if zl % 8 == 0 else zl
        self.nch = zl // self.cz
        self.zp = -(-self.cz // 8) * 8
        self.kk = yl * self.zp
        cz, nch = self.cz, self.nch
        base = lambda s: (s + 7) // 8 - 4
        self.base_p = [base(zl * p) for p in range(npz)]
        starts = np.array([[zl * p + cz * c for c in range(nch)] for p in range(npz)])
        bases = base(starts)
        self.nic = int(np.max((starts + cz - 1) // 8 - bases + 1))
        self.offs = bases - bases[:, :1]
        self.ni = int(self.offs.max()) + self.nic
        self.groups = -(-self.ni // self.pk)
        z = starts[:, :, None, None] + np.arange(cz)[None, None, None, :]
        i = bases[:, :, None, None] + np.arange(8)[None, None, :, None]
        az = np.where((i >= 0) & (i < self.oz), tap(z - 16 - 8 * i), 0.0)
        az[:, :, self.nic:] = 0.0
        az = np.pad(az, ((0, 0), (0, 0), (0, 0), (0, self.zp - cz)))
        self.az = np.tile(az, (1, 1, 1, yl)).astype(np.float32)
        ay = np.zeros((npy, 8, yl))
        self.mask = np.zeros((npy, self.oy // 8, 8), np.float32)
        for d in range(npy):
            y = yl * d + np.arange(yl)
            for j in range(self.oy):
                w = tap(y - 16 - 8 * j)
                if np.any(w != 0):
                    ay[d, j % 8] += w
                    self.mask[d, j // 8, j % 8] = 1.0
        assert self.mask.sum(axis=1).max() == 1
        self.ay = np.repeat(ay, self.zp, axis=2).astype(np.float32)
        n = np.arange(self.nx)[:, None]
        k = np.arange(self.ox)[None, :]
        t = (n - 8 * k + self.nx // 2) % self.nx - self.nx // 2
        wx = tap(t).astype(np.float32)
        self.wx_hi = wx.astype(ml_dtypes.bfloat16)
        self.wx_lo = (wx - self.wx_hi.astype(np.float32)).astype(ml_dtypes.bfloat16)


def split(val):
    hi = val.astype(bf16)
    return hi, (val - hi.astype(f32)).astype(bf16)


def dot(a, b):
    return jnp.dot(a, b, preferred_element_type=f32)


def sum_block(pn, c, p, d, v_ref, az_ref, ay_ref, acc):
    xt = 256
    wz = az_ref[p, c][: pn.nic]
    wy = ay_ref[d]
    w = (wz[:, None, :] * wy[None, :, :]).reshape(pn.nic * 8, pn.kk)
    w_hi = w.astype(bf16).astype(f32)
    w2 = jnp.concatenate([w_hi, w - w_hi], axis=0).astype(bf16)
    off = (pn.zl * p + pn.cz * c + 7) // 8 - (pn.zl * p + 7) // 8
    m = pn.nic * 8

    def tile(x, carry):
        xs = pl.ds(pl.multiple_of(x * xt, xt), xt)
        comps = []
        for a in range(3):
            blk = v_ref[a, :, :, xs]
            if pn.zp > pn.cz:
                blk = jnp.concatenate([blk, jnp.zeros((pn.yl, pn.zp - pn.cz, xt), f32)], axis=1)
            comps.append(blk.reshape(pn.kk, xt))
        for f in range(9):
            if f < 3:
                val = comps[f]
            else:
                a, b = stress_pairs[f - 3]
                val = comps[a] * comps[b]
            hi, lo = split(val)
            r = dot(w2, hi) + dot(w2, lo)
            r = (r[:m] + r[m:]).reshape(pn.nic, 8, xt)
            acc[f, pl.ds(off, pn.nic), :, xs] += r
        return carry

    lax.fori_loop(0, pn.nx // xt, tile, 0)


def first_group(pn, g, acc, wh_ref, wl_ref, out_ref):
    rows = min(pn.pk, pn.ni - g * pn.pk)
    parts = []
    for q in range(rows):
        a = acc[:, g * pn.pk + q].reshape(72, pn.nx)
        hi, lo = split(a)
        parts.append(dot(hi, wh_ref[...]) + (dot(lo, wh_ref[...]) + dot(hi, wl_ref[...])))
    lane = lax.broadcasted_iota(jnp.int32, (72, 128), 1)
    for m in range(pn.npy):
        mg, mo = divmod(m * pn.kb, 128)
        res = jnp.zeros((72, 128), f32)
        for q in range(rows):
            piece = parts[q][:, mg * 128:(mg + 1) * 128]
            shift = (q * pn.kb - mo) % 128
            if shift:
                piece = pltpu.roll(piece, shift, 1)
            res = jnp.where((lane >= q * pn.kb) & (lane < (q + 1) * pn.kb), piece, res)
        out_ref[m, g] = res.reshape(9, 8, 128)


def local_kernel(pn, v_ref, az_ref, ay_ref, wh_ref, wl_ref, out_ref, acc):
    c = pl.program_id(0)
    d, p = lax.axis_index("py"), lax.axis_index("pz")

    @pl.when(c == 0)
    def _():
        acc[...] = jnp.zeros_like(acc)

    sum_block(pn, c, p, d, v_ref, az_ref, ay_ref, acc)

    @pl.when(c == pn.nch - 1)
    def _():
        for g in range(pn.groups):
            first_group(pn, g, acc, wh_ref, wl_ref, out_ref)


def local_sums(pn, velocity):
    whole = lambda a: pl.BlockSpec(a.shape, lambda c: (0,) * a.ndim)
    tables = [pn.az, pn.ay, pn.wx_hi, pn.wx_lo]
    return pl.pallas_call(
        functools.partial(local_kernel, pn),
        grid=(pn.nch,),
        in_specs=[pl.BlockSpec((3, pn.yl, pn.cz, pn.nx), lambda c: (0, 0, c, 0))] + [whole(t) for t in tables],
        out_specs=pl.BlockSpec((pn.npy, pn.groups, 9, 8, 128), lambda c: (0, 0, 0, 0, 0)),
        out_shape=jax.ShapeDtypeStruct((pn.npy, pn.groups, 9, 8, 128), f32),
        scratch_shapes=[pltpu.VMEM((9, pn.ni, 8, pn.nx), f32)],
        compiler_params=pltpu.CompilerParams(vmem_limit_bytes=50 * 2**20),
    )(velocity, *[jnp.asarray(t) for t in tables])


def exchange_kernel(pn, in_ref, vel_ref, str_ref, rec_y, snd_z, rec_z, sy, ry, sz, rz):
    d, p = lax.axis_index("py"), lax.axis_index("pz")
    npy, npz, jq, kb = pn.npy, pn.npz, pn.jq, pn.kb
    mesh_id = pl.DeviceIdType.MESH
    barrier = pltpu.get_barrier_semaphore()
    for o in range(1, npy):
        pl.semaphore_signal(barrier, inc=1, device_id=(lax.rem(d + o, npy), p), device_id_type=mesh_id)
    for o in range(1, npz):
        pl.semaphore_signal(barrier, inc=1, device_id=(d, lax.rem(p + o, npz)), device_id_type=mesh_id)
    pl.semaphore_wait(barrier, npy + npz - 2)

    y_copies = []
    for g in range(pn.groups):
        y_copies.append([])
        for o in range(1, npy):
            to = lax.rem(d + o, npy)
            copy = pltpu.make_async_remote_copy(
                src_ref=in_ref.at[to, g], dst_ref=rec_y.at[d, g], send_sem=sy.at[g, o], recv_sem=ry.at[g, o],
                device_id=(to, p), device_id_type=mesh_id)
            copy.start()
            y_copies[g].append(copy)
    rec_y[d] = in_ref[d]
    z_copies = []

    row = lax.broadcasted_iota(jnp.int32, (9, 8, 128), 1)
    for g in range(pn.groups):
        for copy in y_copies[g]:
            copy.wait()
        for h in range(pn.oy // 8):
            total = jnp.zeros((9, 8, 128), f32)
            for s in range(npy):
                rows = np.nonzero(pn.mask[s, h])[0]
                if len(rows) == 0:
                    continue
                val = rec_y[s, g]
                if len(rows) < 8:
                    val = jnp.where((row >= int(rows[0])) & (row <= int(rows[-1])), val, 0.0)
                total = total + val
            for part in range(8 // jq):
                snd_z[h * (8 // jq) + part, g] = total[:, part * jq:(part + 1) * jq, :]
        for o in range(1, npz):
            to = lax.rem(p + o, npz)
            copy = pltpu.make_async_remote_copy(
                src_ref=snd_z.at[to, g], dst_ref=rec_z.at[p, g], send_sem=sz.at[g, o], recv_sem=rz.at[g, o],
                device_id=(d, to), device_id_type=mesh_id)
            copy.start()
            z_copies.append(copy)
    rec_z[p] = snd_z[p]
    for copy in z_copies:
        copy.wait()

    for i in range(pn.oz):
        total = jnp.zeros((9, jq, kb), f32)
        for s in range(npz):
            n = i - pn.base_p[s]
            if 0 <= n < pn.ni:
                g, q = divmod(n, pn.pk)
                total = total + rec_z[s, g, :, :, q * kb:(q + 1) * kb]
        vel_ref[:, i] = total[:3]
        for n, (a, b) in enumerate(stress_pairs):
            str_ref[n, i] = total[3 + n] - total[a] * total[b]


def exchange(pn, packed):
    vmem = pl.BlockSpec(memory_space=pltpu.VMEM)
    zbuf = pltpu.VMEM((pn.npz, pn.groups, 9, pn.jq, 128), f32)
    sems = [pltpu.SemaphoreType.DMA((pn.groups, n)) for n in (pn.npy, pn.npy, pn.npz, pn.npz)]
    return pl.pallas_call(
        functools.partial(exchange_kernel, pn),
        in_specs=[vmem],
        out_specs=(vmem, vmem),
        out_shape=tuple(jax.ShapeDtypeStruct((n, pn.oz, pn.jq, pn.kb), f32) for n in (3, 6)),
        scratch_shapes=[pltpu.VMEM((pn.npy, pn.groups, 9, 8, 128), f32), zbuf, zbuf] + sems,
        compiler_params=pltpu.CompilerParams(
            collective_id=0, has_side_effects=True, vmem_limit_bytes=32 * 2**20
        ),
    )(packed)


def on_device(npy, npz, velocity):
    pn = Plan(velocity.shape, npy, npz)
    packed = local_sums(pn, jnp.transpose(velocity, (0, 2, 1, 3)))
    return exchange(pn, packed)


def solution(mesh):
    return jax.shard_map(
        functools.partial(on_device, mesh.shape["py"], mesh.shape["pz"]),
        mesh=mesh,
        in_specs=(P(None, "pz", "py", None),),
        out_specs=(P(None, None, "pz", "py"), P(None, None, "pz", "py")),
        check_vma=False,
    )
```

```python
import functools
import numpy as np
import ml_dtypes
import jax
import jax.numpy as jnp
from jax import lax
from jax.sharding import PartitionSpec as P
from jax.experimental import pallas as pl
from jax.experimental.pallas import tpu as pltpu

stress_pairs = ((0, 0), (0, 1), (0, 2), (1, 1), (1, 2), (2, 2))
f32, bf16 = jnp.float32, jnp.bfloat16


def tap(t):
    r = np.arange(-16, 17).astype(np.float64)
    s = np.sum(np.exp(-r * r / 128.0))
    t = np.asarray(t, np.float64)
    return np.where(np.abs(t) <= 16, np.exp(-t * t / 128.0) / s, 0.0)


class Plan:
    def __init__(self, shape, npy, npz):
        _, self.zl, self.yl, self.nx = shape
        self.npy, self.npz = npy, npz
        zl, yl = self.zl, self.yl
        self.oz = (zl * npz - 32) // 8
        self.oy = (yl * npy - 32) // 8
        self.ox = self.nx // 8
        self.kb = self.ox // npy
        self.jq = self.oy // npz
        self.pk = 128 // self.kb
        self.cz = 8 if zl % 8 == 0 else zl
        self.nch = zl // self.cz
        self.zp = -(-self.cz // 8) * 8
        self.kk = yl * self.zp
        cz, nch = self.cz, self.nch
        base = lambda s: (s + 7) // 8 - 4
        self.base_p = [base(zl * p) for p in range(npz)]
        starts = np.array([[zl * p + cz * c for c in range(nch)] for p in range(npz)])
        bases = base(starts)
        self.nic = int(np.max((starts + cz - 1) // 8 - bases + 1))
        self.offs = bases - bases[:, :1]
        self.ni = int(self.offs.max()) + self.nic
        self.groups = -(-self.ni // self.pk)
        z = starts[:, :, None, None] + np.arange(cz)[None, None, None, :]
        i = bases[:, :, None, None] + np.arange(8)[None, None, :, None]
        az = np.where((i >= 0) & (i < self.oz), tap(z - 16 - 8 * i), 0.0)
        az[:, :, self.nic:] = 0.0
        az = np.pad(az, ((0, 0), (0, 0), (0, 0), (0, self.zp - cz)))
        self.az = np.tile(az, (1, 1, 1, yl)).astype(np.float32)
        ay = np.zeros((npy, 8, yl))
        self.mask = np.zeros((npy, self.oy // 8, 8), np.float32)
        for d in range(npy):
            y = yl * d + np.arange(yl)
            for j in range(self.oy):
                w = tap(y - 16 - 8 * j)
                if np.any(w != 0):
                    ay[d, j % 8] += w
                    self.mask[d, j // 8, j % 8] = 1.0
        assert self.mask.sum(axis=1).max() == 1
        self.ay = np.repeat(ay, self.zp, axis=2).astype(np.float32)
        n = np.arange(self.nx)[:, None]
        k = np.arange(self.ox)[None, :]
        t = (n - 8 * k + self.nx // 2) % self.nx - self.nx // 2
        wx = tap(t).astype(np.float32)
        self.wx_hi = wx.astype(ml_dtypes.bfloat16)
        self.wx_lo = (wx - self.wx_hi.astype(np.float32)).astype(ml_dtypes.bfloat16)


def split(val):
    hi = val.astype(bf16)
    return hi, (val - hi.astype(f32)).astype(bf16)


def dot(a, b):
    return jnp.dot(a, b, preferred_element_type=f32)


def sum_block(pn, c, p, d, v_ref, az_ref, ay_ref, acc):
    xt = 512
    wz = az_ref[p, c][: pn.nic]
    wy = ay_ref[d]
    w = (wz[:, None, :] * wy[None, :, :]).reshape(pn.nic * 8, pn.kk)
    w_hi = w.astype(bf16).astype(f32)
    w2 = jnp.concatenate([w_hi, w - w_hi], axis=0).astype(bf16)
    off = (pn.zl * p + pn.cz * c + 7) // 8 - (pn.zl * p + 7) // 8
    m = pn.nic * 8

    def tile(x, carry):
        xs = pl.ds(pl.multiple_of(x * xt, xt), xt)
        comps = []
        for a in range(3):
            blk = v_ref[a, :, :, xs]
            if pn.zp > pn.cz:
                blk = jnp.concatenate([blk, jnp.zeros((pn.yl, pn.zp - pn.cz, xt), f32)], axis=1)
            comps.append(blk.reshape(pn.kk, xt))
        for f in range(9):
            if f < 3:
                val = comps[f]
            else:
                a, b = stress_pairs[f - 3]
                val = comps[a] * comps[b]
            hi, lo = split(val)
            r = dot(w2, hi) + dot(w2, lo)
            r = (r[:m] + r[m:]).reshape(pn.nic, 8, xt)
            acc[f, pl.ds(off, pn.nic), :, xs] += r
        return carry

    lax.fori_loop(0, pn.nx // xt, tile, 0)


def first_group(pn, g, acc, wh_ref, wl_ref, out_ref):
    rows = min(pn.pk, pn.ni - g * pn.pk)
    parts = []
    for q in range(rows):
        a = acc[:, g * pn.pk + q].reshape(72, pn.nx)
        hi, lo = split(a)
        parts.append(dot(hi, wh_ref[...]) + (dot(lo, wh_ref[...]) + dot(hi, wl_ref[...])))
    lane = lax.broadcasted_iota(jnp.int32, (72, 128), 1)
    for m in range(pn.npy):
        mg, mo = divmod(m * pn.kb, 128)
        res = jnp.zeros((72, 128), f32)
        for q in range(rows):
            piece = parts[q][:, mg * 128:(mg + 1) * 128]
            shift = (q * pn.kb - mo) % 128
            if shift:
                piece = pltpu.roll(piece, shift, 1)
            res = jnp.where((lane >= q * pn.kb) & (lane < (q + 1) * pn.kb), piece, res)
        out_ref[m, g] = res.reshape(9, 8, 128)


def local_kernel(pn, v_ref, az_ref, ay_ref, wh_ref, wl_ref, out_ref, acc):
    c = pl.program_id(0)
    d, p = lax.axis_index("py"), lax.axis_index("pz")

    @pl.when(c == 0)
    def _():
        acc[...] = jnp.zeros_like(acc)

    sum_block(pn, c, p, d, v_ref, az_ref, ay_ref, acc)

    @pl.when(c == pn.nch - 1)
    def _():
        for g in range(pn.groups):
            first_group(pn, g, acc, wh_ref, wl_ref, out_ref)


def local_sums(pn, velocity):
    whole = lambda a: pl.BlockSpec(a.shape, lambda c: (0,) * a.ndim)
    tables = [pn.az, pn.ay, pn.wx_hi, pn.wx_lo]
    return pl.pallas_call(
        functools.partial(local_kernel, pn),
        grid=(pn.nch,),
        in_specs=[pl.BlockSpec((3, pn.yl, pn.cz, pn.nx), lambda c: (0, 0, c, 0))] + [whole(t) for t in tables],
        out_specs=pl.BlockSpec((pn.npy, pn.groups, 9, 8, 128), lambda c: (0, 0, 0, 0, 0)),
        out_shape=jax.ShapeDtypeStruct((pn.npy, pn.groups, 9, 8, 128), f32),
        scratch_shapes=[pltpu.VMEM((9, pn.ni, 8, pn.nx), f32)],
        compiler_params=pltpu.CompilerParams(vmem_limit_bytes=50 * 2**20),
    )(velocity, *[jnp.asarray(t) for t in tables])


def exchange_kernel(pn, in_ref, vel_ref, str_ref, rec_y, snd_z, rec_z, sy, ry, sz, rz):
    d, p = lax.axis_index("py"), lax.axis_index("pz")
    npy, npz, jq, kb = pn.npy, pn.npz, pn.jq, pn.kb
    mesh_id = pl.DeviceIdType.MESH
    barrier = pltpu.get_barrier_semaphore()
    for o in range(1, npy):
        pl.semaphore_signal(barrier, inc=1, device_id=(lax.rem(d + o, npy), p), device_id_type=mesh_id)
    for o in range(1, npz):
        pl.semaphore_signal(barrier, inc=1, device_id=(d, lax.rem(p + o, npz)), device_id_type=mesh_id)
    pl.semaphore_wait(barrier, npy + npz - 2)

    y_copies = []
    for g in range(pn.groups):
        y_copies.append([])
        for o in range(1, npy):
            to = lax.rem(d + o, npy)
            copy = pltpu.make_async_remote_copy(
                src_ref=in_ref.at[to, g], dst_ref=rec_y.at[d, g], send_sem=sy.at[g, o], recv_sem=ry.at[g, o],
                device_id=(to, p), device_id_type=mesh_id)
            copy.start()
            y_copies[g].append(copy)
    rec_y[d] = in_ref[d]
    z_copies = []

    row = lax.broadcasted_iota(jnp.int32, (9, 8, 128), 1)
    for g in range(pn.groups):
        for copy in y_copies[g]:
            copy.wait()
        for h in range(pn.oy // 8):
            total = jnp.zeros((9, 8, 128), f32)
            for s in range(npy):
                rows = np.nonzero(pn.mask[s, h])[0]
                if len(rows) == 0:
                    continue
                val = rec_y[s, g]
                if len(rows) < 8:
                    val = jnp.where((row >= int(rows[0])) & (row <= int(rows[-1])), val, 0.0)
                total = total + val
            for part in range(8 // jq):
                snd_z[h * (8 // jq) + part, g] = total[:, part * jq:(part + 1) * jq, :]
        for o in range(1, npz):
            to = lax.rem(p + o, npz)
            copy = pltpu.make_async_remote_copy(
                src_ref=snd_z.at[to, g], dst_ref=rec_z.at[p, g], send_sem=sz.at[g, o], recv_sem=rz.at[g, o],
                device_id=(d, to), device_id_type=mesh_id)
            copy.start()
            z_copies.append(copy)
    rec_z[p] = snd_z[p]
    for copy in z_copies:
        copy.wait()

    for i in range(pn.oz):
        total = jnp.zeros((9, jq, kb), f32)
        for s in range(npz):
            n = i - pn.base_p[s]
            if 0 <= n < pn.ni:
                g, q = divmod(n, pn.pk)
                total = total + rec_z[s, g, :, :, q * kb:(q + 1) * kb]
        vel_ref[:, i] = total[:3]
        for n, (a, b) in enumerate(stress_pairs):
            str_ref[n, i] = total[3 + n] - total[a] * total[b]


def exchange(pn, packed):
    vmem = pl.BlockSpec(memory_space=pltpu.VMEM)
    zbuf = pltpu.VMEM((pn.npz, pn.groups, 9, pn.jq, 128), f32)
    sems = [pltpu.SemaphoreType.DMA((pn.groups, n)) for n in (pn.npy, pn.npy, pn.npz, pn.npz)]
    return pl.pallas_call(
        functools.partial(exchange_kernel, pn),
        in_specs=[vmem],
        out_specs=(vmem, vmem),
        out_shape=tuple(jax.ShapeDtypeStruct((n, pn.oz, pn.jq, pn.kb), f32) for n in (3, 6)),
        scratch_shapes=[pltpu.VMEM((pn.npy, pn.groups, 9, 8, 128), f32), zbuf, zbuf] + sems,
        compiler_params=pltpu.CompilerParams(
            collective_id=0, has_side_effects=True, vmem_limit_bytes=32 * 2**20
        ),
    )(packed)


def on_device(npy, npz, velocity):
    pn = Plan(velocity.shape, npy, npz)
    packed = local_sums(pn, jnp.transpose(velocity, (0, 2, 1, 3)))
    return exchange(pn, packed)


def solution(mesh):
    return jax.shard_map(
        functools.partial(on_device, mesh.shape["py"], mesh.shape["pz"]),
        mesh=mesh,
        in_specs=(P(None, "pz", "py", None),),
        out_specs=(P(None, None, "pz", "py"), P(None, None, "pz", "py")),
        check_vma=False,
    )
```
